32 devices in a mesh: illum: 16 (over z, y, x), row: 2 (over core).
Axes of the slice: x: 2, y: 2, z: 4, core: 2. Of those that a mesh axis runs over, the one named last changes fastest.
Arguments:
- angles: int32 [64, 2], P('illum'), may hold values from -8 to 8
- depth_order: int32 [3], replicated, may hold values from 0 to 15, as said below
- slices: float32 [16, 16, 4096], P('illum', 'row'), may hold values from -4 to 4
- cotangent: float32 [64, 2, 16, 4096], P('illum', None, 'row'), may hold values from -0.6 to 0.6
Outputs:
- exit_field: float32 [64, 2, 16, 4096], P('illum', None, 'row')
- slice_grad: float32 [16, 16, 4096], P('illum', 'row')
The draws below stay inside these ranges and needn't reach their ends.
Inputs may be any that keep to these rules, and one draw needn't show every extreme that they name: `depth_order`: 3 distinct slice numbers; slice 0 and the last slice are always among them.
All inputs are finite; a program needn't handle non-finite values.
Results may differ from the reference program's by a relative error of at most 0.0001.
Values sent between devices are 32-bit elements; how exact they have to be, the bound alone decides.
A program may use at most 64 MiB of HBM per device.

```python
import math
import jax
import jax.numpy as jnp

NY = 4096
LAYERS = 3
NX = 16
ILLUMS = 64
SLICES = 16
N_ILLUM = 16


def draw_depth_order(key, part):
    first_key = jax.random.fold_in(key, 11)
    second_key = jax.random.fold_in(key, 23)
    middle = 1 + jax.random.permutation(first_key, SLICES - 2)[:LAYERS - 2].astype(jnp.int32)
    values = jnp.concatenate([jnp.zeros((1,), jnp.int32), middle, jnp.full((1,), SLICES - 1, jnp.int32)])
    order = jax.random.permutation(second_key, LAYERS)
    return values[order].astype(jnp.int32)


def place_ends(drawn, own_key, low, largest):
    extent = drawn.shape
    index_at = [jax.random.randint(jax.random.fold_in(own_key, axis), (), 0, extent[axis]) for axis in range(len(extent))]
    drawn = drawn.at[tuple(index_at)].set(low)
    longest = extent.index(max(extent))
    index_at[longest] = (index_at[longest] + 1) % extent[longest]
    return drawn.at[tuple(index_at)].set(largest)


def levels(own_key, extent, split, low, top_value):
    def one(axis_at, shards_of):
        draws = jax.random.uniform(jax.random.fold_in(jax.random.fold_in(own_key, 6), axis_at), (shards_of,), jnp.float32, low / len(split), top_value / len(split))
        return jnp.repeat(jnp.exp(draws), extent[axis_at] // shards_of).reshape((-1,) + (1,) * (len(extent) - axis_at - 1))

    level = one(*split[0])
    for cut in split[1:]:
        level = level * one(*cut)
    return level


def normal_values(own_key, extent, deviation, reach, split=(), held_as=jnp.bfloat16):
    level = levels(own_key, extent, split, -0.22, 0.18) if split else 1.0
    entries = jax.random.normal(own_key, extent, jnp.float32) * deviation * level
    return jnp.minimum(jnp.maximum(entries, -reach), reach).astype(held_as)


def setup_inputs(seed: int = 0) -> dict:
    seeds = jax.random.split(jax.random.key(seed), 5)
    angles = place_ends(jax.random.randint(seeds[0], (ILLUMS, 2), -8, 9), jax.random.fold_in(seeds[0], 1), -8, 8).astype(jnp.int32)
    depth_order = draw_depth_order(jax.random.fold_in(seeds[4], 71), 0)
    slices = normal_values(seeds[2], (SLICES, NX, NY), 1.0, 4.0, ((0, 16), (1, 2)), jnp.float32)
    cotangent = normal_values(seeds[3], (ILLUMS, 2, NX, NY), 0.1, 0.6, ((0, 16), (2, 2)), jnp.float32)
    return dict(angles=angles, depth_order=depth_order, slices=slices, cotangent=cotangent)


rate_scale = 0.3


def laplace(field):
    padded = jnp.pad(field, [(0, 0)] * (field.ndim - 2) + [(1, 1), (1, 1)])
    return (padded[..., 2:, 1:-1] + padded[..., :-2, 1:-1]) + (padded[..., 1:-1, 2:] + padded[..., 1:-1, :-2]) - 4.0 * field


def rate(field, factor):
    curved = laplace(field)
    return jnp.stack([-factor * curved[:, 1], factor * curved[:, 0]], axis=1)


def runge_step(field, factor):
    slope_one = rate(field, factor)
    slope_two = rate(field + 0.5 * slope_one, factor)
    slope_three = rate(field + 0.5 * slope_two, factor)
    slope_four = rate(field + slope_three, factor)
    return field + (slope_one + 2.0 * slope_two + 2.0 * slope_three + slope_four) / 6.0


def rotate(field, phase):
    cosine = jnp.cos(phase)
    sine = jnp.sin(phase)
    real_part = field[:, 0]
    imag_part = field[:, 1]
    return jnp.stack([cosine * real_part - sine * imag_part, sine * real_part + cosine * imag_part], axis=1)


def reference(angles, depth_order, slices, cotangent):
    rows_idx = jnp.arange(NX, dtype=jnp.int32)
    cols_idx = jnp.arange(NY, dtype=jnp.int32)
    phase_rows = 2.0 * math.pi * ((angles[:, 0:1] * rows_idx[None, :]) % NX).astype(jnp.float32) / NX
    phase_cols = 2.0 * math.pi * ((angles[:, 1:2] * cols_idx[None, :]) % NY).astype(jnp.float32) / NY
    phase = phase_rows[:, :, None] + phase_cols[:, None, :]
    field = jnp.stack([jnp.cos(phase), jnp.sin(phase)], axis=1)
    kept = []
    chosen = []
    for layer in range(LAYERS):
        plane = slices[depth_order[layer]]
        chosen.append(plane)
        field = rotate(field, plane)
        kept.append(field)
        field = runge_step(field, rate_scale)
    exit_field = field
    adjoint = cotangent
    owners = jnp.arange(N_ILLUM, dtype=jnp.int32)
    slice_grad = jnp.zeros((N_ILLUM, NX, NY), jnp.float32)
    for layer in range(LAYERS - 1, -1, -1):
        adjoint = runge_step(adjoint, -rate_scale)
        stored = kept[layer]
        term = jnp.sum(-adjoint[:, 0] * stored[:, 1] + adjoint[:, 1] * stored[:, 0], axis=0)
        picked = (owners == depth_order[layer]).astype(jnp.float32)
        slice_grad = slice_grad + picked[:, None, None] * term[None]
        adjoint = rotate(adjoint, -chosen[layer])
    return exit_field, slice_grad
```

```python
import functools
import math

import jax
import jax.numpy as jnp
from jax import lax
from jax.experimental import pallas as pl
from jax.experimental.pallas import tpu as pltpu
from jax.sharding import PartitionSpec as P

rate_scale = 0.3


def extended(array, sides, width):
    for axis, dim in sides:
        peers, length = (lax.axis_size(axis), array.shape[dim])
        up = [(i, (i + 1) % peers) for i in range(peers - 1)]
        down = [(j, i) for i, j in up]
        last = lax.slice_in_dim(array, length - width, length, axis=dim)
        initial = lax.slice_in_dim(array, 0, width, axis=dim)
        before = lax.ppermute(last, axis, up)
        after = lax.ppermute(initial, axis, down)
        array = jnp.concatenate([before, array, after], axis=dim)
    return array


def broadcast(block, axis, holder):
    block = jnp.where(lax.axis_index(axis) == holder, block, jnp.zeros_like(block))
    return lax.psum(block, axis)


def laplace_whole(field):
    framed = jnp.pad(field, ((0, 0), (0, 0), (1, 1), (1, 1)))
    return (
        framed[:, :, 2:, 1:-1]
        + framed[:, :, :-2, 1:-1]
        + (framed[:, :, 1:-1, 2:] + framed[:, :, 1:-1, :-2])
        - 4.0 * field
    )


def deep_runge(field, factor, valid):
    padded = extended(field, (("row", 2),), 4)

    def slope(state):
        curved = laplace_whole(state)
        return jnp.stack([-factor * curved[:, 1], factor * curved[:, 0]], axis=1) * valid

    slope_one = slope(padded)
    slope_two = slope(padded + 0.5 * slope_one)
    slope_three = slope(padded + 0.5 * slope_two)
    slope_four = slope(padded + slope_three)
    total = padded + (slope_one + 2.0 * slope_two + 2.0 * slope_three + slope_four) / 6.0
    return total[:, :, 4:-4]


def rotate(field, phase):
    cosine = jnp.cos(phase)
    sine = jnp.sin(phase)
    real_part = field[:, 0]
    imag_part = field[:, 1]
    return jnp.stack(
        [cosine * real_part - sine * imag_part, sine * real_part + cosine * imag_part], axis=1
    )


def inner_term(adjoint, stored):
    return jnp.sum(-adjoint[:, 0] * stored[:, 1] + adjoint[:, 1] * stored[:, 0], axis=0)


def body(angles, depth_order, slices, cotangent):
    rows = slices.shape[1]
    cols = slices.shape[2]
    layers = depth_order.shape[0]
    owner_count = lax.axis_size("illum")
    total_rows = rows * lax.axis_size("row")
    first_row = lax.axis_index("row") * rows
    rows_idx = first_row + jnp.arange(rows, dtype=jnp.int32)
    cols_idx = jnp.arange(cols, dtype=jnp.int32)
    phase_rows = (
        2.0
        * math.pi
        * (angles[:, 0:1] * rows_idx[None, :] % total_rows).astype(jnp.float32)
        / total_rows
    )
    phase_cols = (
        2.0 * math.pi * (angles[:, 1:2] * cols_idx[None, :] % cols).astype(jnp.float32) / cols
    )
    phase = phase_rows[:, :, None] + phase_cols[:, None, :]
    field = jnp.stack([jnp.cos(phase), jnp.sin(phase)], axis=1)
    chosen = [broadcast(slices[0], "illum", depth_order[layer]) for layer in range(layers)]
    kept = [None] * layers
    terms = [None] * layers
    adjoint = cotangent
    wide_idx = first_row - 4 + jnp.arange(rows + 8, dtype=jnp.int32)
    valid = ((wide_idx >= 0) & (wide_idx < total_rows)).astype(jnp.float32)[:, None]
    for layer in range(layers):
        field = rotate(field, chosen[layer])
        kept[layer] = field
        field = deep_runge(field, rate_scale, valid)
    for layer in range(layers - 1, -1, -1):
        adjoint = deep_runge(adjoint, -rate_scale, valid)
        terms[layer] = inner_term(adjoint, kept[layer])
        adjoint = rotate(adjoint, -chosen[layer])
    grads = jnp.stack(terms, axis=0)
    owners = jnp.arange(owner_count, dtype=jnp.int32)
    buffer = jnp.zeros((owner_count, rows, cols), jnp.float32)
    for layer in range(layers):
        picked = (owners == depth_order[layer]).astype(jnp.float32)
        buffer = buffer + picked[:, None, None] * grads[layer][None]
    slice_grad = lax.psum_scatter(buffer, "illum", scatter_dimension=0, tiled=True)
    return (field, slice_grad)


MESH = pl.DeviceIdType.MESH
PAD = 128
STRIP = 512


def sincos(x):
    k = jnp.floor(x * (2.0 / math.pi) + 0.5)
    r = x - k * 1.5703125
    r = r - k * 4.837512969970703125e-4
    r = r - k * 7.54978995489188e-8
    z = r * r
    s = r + r * z * (-1.6666654611e-1 + z * (8.3321608736e-3 - z * 1.9515295891e-4))
    c = 1.0 - 0.5 * z + z * z * (
        4.166664568298827e-2 + z * (-1.388731625493765e-3 + z * 2.443315711809948e-5)
    )
    q = k.astype(jnp.int32) & 3
    odd = (q & 1) == 1
    sin_mag = jnp.where(odd, c, s)
    cos_mag = jnp.where(odd, s, c)
    sine = jnp.where(q >= 2, -sin_mag, sin_mag)
    cosine = jnp.where((q == 1) | (q == 2), -cos_mag, cos_mag)
    return sine, cosine


def propagate(source, target, g, factor, cols):
    wide = STRIP + 2 * PAD
    sub = lax.broadcasted_iota(jnp.int32, (8, wide), 0)
    lane = lax.broadcasted_iota(jnp.int32, (8, wide), 1)
    first, final = sub == 0, sub == 7
    second = factor * factor / 2.0
    third = factor * factor * factor / 6.0
    fourth = factor * factor * factor * factor / 24.0
    mid = slice(PAD, PAD + STRIP)

    def strip(j, carry):
        start = pl.multiple_of(j * STRIP, STRIP)
        col = lane + (start - PAD)
        inside = jnp.where((col >= 0) & (col < cols), 1.0, 0.0).astype(jnp.float32)

        def curved(t, b):
            rt, rb = pltpu.roll(t, 1, 0), pltpu.roll(b, 1, 0)
            qt, qb = pltpu.roll(t, 7, 0), pltpu.roll(b, 7, 0)
            vt = jnp.where(first, 0.0, rt) + jnp.where(final, qb, qt)
            vb = jnp.where(first, rt, rb) + jnp.where(final, 0.0, qb)
            ht = pltpu.roll(t, 1, 1) + pltpu.roll(t, wide - 1, 1)
            hb = pltpu.roll(b, 1, 1) + pltpu.roll(b, wide - 1, 1)
            return (vt + ht) - 4.0 * t, (vb + hb) - 4.0 * b

        evens, odds = [], []
        for part in range(2):
            u0 = source[g, part, 0:8, pl.ds(start, wide)]
            u1 = source[g, part, 8:16, pl.ds(start, wide)]
            a0, a1 = curved(u0, u1)
            a0, a1 = a0 * inside, a1 * inside
            b0, b1 = curved(a0, a1)
            b0, b1 = b0 * inside, b1 * inside
            even = [u[:, mid] - second * b[:, mid] for u, b in ((u0, b0), (u1, b1))]
            c0, c1 = curved(b0, b1)
            c0, c1 = c0 * inside, c1 * inside
            odd = [factor * a[:, mid] - third * c[:, mid] for a, c in ((a0, c0), (a1, c1))]
            d0, d1 = curved(c0, c1)
            even = [e + fourth * d[:, mid] for e, d in zip(even, (d0, d1))]
            evens.append(even)
            odds.append(odd)
        for half in range(2):
            at = slice(8 * half, 8 * half + 8)
            target[g, 0, at, pl.ds(start, STRIP)] = evens[0][half] - odds[1][half]
            target[g, 1, at, pl.ds(start, STRIP)] = evens[1][half] + odds[0][half]
        return carry

    lax.fori_loop(0, cols // STRIP, strip, 0)


def fused(
    count, angles, order, slices, cot, out, grad,
    tmp, w2, w1, w0, field, full, sine, cosine, term, got, total, parts, rs, picks, gfull, pieces,
    cot_send, cot_recv, cot_local, a2a_send, a2a_recv, ag_send, ag_recv, cx_send, cx_recv,
    tx_send, tx_recv, rs_send, rs_recv, fin_send, fin_recv, ex_send, ex_recv, ex_local,
):
    n = count
    me = lax.axis_index("illum")
    core = lax.axis_index("row")
    other = 1 - core
    cols = slices.shape[1]
    width = cols // n
    held = cot.shape[0] // 2
    layers = full.shape[0]
    mine_rows = pl.ds(pl.multiple_of(core * 8, 8), 8)
    other_rows = pl.ds(pl.multiple_of(other * 8, 8), 8)
    my_cols = pl.ds(pl.multiple_of(me * width, width), width)

    def peer(k):
        return lax.rem(me + k, n)

    def piece(k):
        return pl.ds(pl.multiple_of(k * width, width), width)

    def loop(body):
        def step(k, carry):
            body(k)
            return carry

        lax.fori_loop(1, n, step, 0)

    barrier = pltpu.get_barrier_semaphore()
    loop(lambda k: pl.semaphore_signal(barrier, inc=1, device_id=(peer(k), core), device_id_type=MESH))
    pl.semaphore_signal(barrier, inc=1, device_id=(me, other), device_id_type=MESH)
    pl.semaphore_wait(barrier, n)

    def remote(src, dst, send, recv, where):
        return pltpu.make_async_remote_copy(
            src_ref=src, dst_ref=dst, send_sem=send, recv_sem=recv,
            device_id=where, device_id_type=MESH,
        )

    inner = pl.ds(PAD, cols)

    def cot_copy(g):
        return remote(
            cot.at[other * held + g], tmp.at[g, :, mine_rows, inner],
            cot_send.at[g], cot_recv.at[g], (me, other),
        )

    def cot_own(g):
        return pltpu.make_async_copy(
            cot.at[core * held + g], tmp.at[g, :, mine_rows, inner], cot_local.at[g]
        )

    def a2a(k):
        return remote(
            slices.at[:, piece(peer(k))], parts.at[me], a2a_send.at[k], a2a_recv.at[k],
            (peer(k), core),
        )

    def gather(layer, k):
        return remote(
            pieces.at[layer], full.at[layer, mine_rows, my_cols],
            ag_send.at[layer, k], ag_recv.at[layer, k], (peer(k), core),
        )

    def cross(layer):
        return remote(
            full.at[layer, mine_rows], full.at[layer, mine_rows],
            cx_send.at[layer], cx_recv.at[layer], (me, other),
        )

    def term_copy(layer):
        return remote(
            term.at[layer, other_rows], got.at[layer],
            tx_send.at[layer], tx_recv.at[layer], (me, other),
        )

    def scatter(layer, k):
        return remote(
            total.at[layer, :, piece(peer(k))], rs.at[layer, k],
            rs_send.at[layer, k], rs_recv.at[layer, k], (peer(k), core),
        )

    def final(k):
        to = peer(k)
        which = (to + n - 2) // (n - 1) + to // (n - 1)
        return remote(
            picks.at[which], gfull.at[:, my_cols], fin_send.at[k], fin_recv.at[k], (to, core)
        )

    def exit_copy(g):
        return remote(
            field.at[g, :, other_rows], out.at[core * held + g],
            ex_send.at[g], ex_recv.at[g], (me, other),
        )

    def exit_own(g):
        return pltpu.make_async_copy(
            field.at[g, :, mine_rows], out.at[core * held + g], ex_local.at[g]
        )

    for g in range(held):
        cot_copy(g).start()
        cot_own(g).start()
    loop(lambda k: a2a(k).start())
    parts[me] = slices[:, my_cols]
    for g in range(held):
        for part in range(2):
            tmp[g, part, :, 0:PAD] = jnp.zeros((16, PAD), jnp.float32)
            tmp[g, part, :, PAD + cols : 2 * PAD + cols] = jnp.zeros((16, PAD), jnp.float32)

    def back_first(g):
        cot_copy(g).wait_recv()
        cot_own(g).wait()
        propagate(tmp, w2, g, -rate_scale, cols)

    back_first(0)
    loop(lambda k: a2a(k).wait_recv())
    for layer in range(layers - 1, -1, -1):
        value = parts[order[layer]]
        pieces[layer] = value
        full[layer, mine_rows, my_cols] = value
        loop(lambda k: gather(layer, k).start())
    for g in range(1, held):
        back_first(g)

    def fetch(layer):
        loop(lambda k: gather(layer, k).wait_recv())
        cross(layer).start()

    tile = 512

    def columns(body):
        def step(j, carry):
            body(pl.multiple_of(j * tile, tile))
            return carry

        lax.fori_loop(0, cols // tile, step, 0)

    def back_turn(layer, waves):
        def body(start):
            at = pl.ds(start, tile)
            to = pl.ds(start + PAD, tile)
            s, c = sincos(full[layer, :, at])
            sine[layer, :, at] = s
            cosine[layer, :, at] = c
            for g in range(held):
                a, b = waves[g, 0, :, at], waves[g, 1, :, at]
                tmp[g, 0, :, to] = a * c + b * s
                tmp[g, 1, :, to] = b * c - a * s

        columns(body)

    fetch(2)
    cross(2).wait_recv()
    fetch(1)
    back_turn(2, w2)
    for g in range(held):
        propagate(tmp, w1, g, -rate_scale, cols)
    cross(1).wait_recv()
    fetch(0)
    back_turn(1, w1)
    for g in range(held):
        propagate(tmp, w0, g, -rate_scale, cols)
    cross(0).wait_recv()

    def first_turn(start):
        at = pl.ds(start, tile)
        to = pl.ds(start + PAD, tile)
        phase = full[0, :, at]
        row = lax.broadcasted_iota(jnp.int32, (16, tile), 0)
        col = lax.broadcasted_iota(jnp.int32, (16, tile), 1) + start
        acc = None
        for g in range(held):
            p = angles[core * held + g, 0]
            q = angles[core * held + g, 1]
            turn = ((row * p) & 15).astype(jnp.float32) * (2.0 * math.pi / 16)
            turn = turn + ((col * q) & (cols - 1)).astype(jnp.float32) * (2.0 * math.pi / cols)
            s, c = sincos(turn + phase)
            tmp[g, 0, :, to] = c
            tmp[g, 1, :, to] = s
            piece_sum = w0[g, 1, :, at] * c - w0[g, 0, :, at] * s
            acc = piece_sum if acc is None else acc + piece_sum
        term[0, :, at] = acc

    def turn(layer, waves):
        def body(start):
            at = pl.ds(start, tile)
            to = pl.ds(start + PAD, tile)
            s, c = sine[layer, :, at], cosine[layer, :, at]
            acc = None
            for g in range(held):
                a, b = field[g, 0, :, at], field[g, 1, :, at]
                real = a * c - b * s
                imag = a * s + b * c
                tmp[g, 0, :, to] = real
                tmp[g, 1, :, to] = imag
                piece_sum = waves[g, 1, :, at] * real - waves[g, 0, :, at] * imag
                acc = piece_sum if acc is None else acc + piece_sum
            term[layer, :, at] = acc

        columns(body)

    def spread(layer):
        term_copy(layer).wait_recv()
        total[layer] = term[layer, mine_rows] + got[layer]
        loop(lambda k: scatter(layer, k).start())

    columns(first_turn)
    term_copy(0).start()
    propagate(tmp, field, 0, rate_scale, cols)
    spread(0)
    for g in range(1, held):
        propagate(tmp, field, g, rate_scale, cols)
    turn(1, w1)
    term_copy(1).start()
    propagate(tmp, field, 0, rate_scale, cols)
    spread(1)
    for g in range(1, held):
        propagate(tmp, field, g, rate_scale, cols)
    turn(2, w2)
    term_copy(2).start()
    propagate(tmp, field, 0, rate_scale, cols)
    spread(2)
    exit_copy(0).start()
    exit_own(0).start()
    for g in range(1, held):
        propagate(tmp, field, g, rate_scale, cols)
        exit_copy(g).start()
        exit_own(g).start()

    sums = []
    for layer in range(layers):
        loop(lambda k: scatter(layer, k).wait_recv())
        acc = total[layer, :, my_cols]
        for k in range(1, n):
            acc = acc + rs[layer, k]
        sums.append(acc)
    zero = jnp.zeros_like(sums[0])
    low = zero
    high = zero
    middle = zero
    for layer in range(layers):
        place = order[layer]
        low = low + jnp.where(place == 0, sums[layer], zero)
        high = high + jnp.where(place == n - 1, sums[layer], zero)
        middle = middle + jnp.where((place > 0) & (place < n - 1), sums[layer], zero)
    picks[0] = low
    picks[1] = middle
    picks[2] = high
    loop(lambda k: final(k).start())
    gfull[:, my_cols] = picks[(me + n - 2) // (n - 1) + me // (n - 1)]
    named = (order[0] == me) | (order[1] == me) | (order[2] == me)
    loop(lambda k: final(k).wait_recv())
    value = gfull[...]
    grad[...] = jnp.where(named, value, jnp.zeros_like(value))

    for g in range(held):
        cot_copy(g).wait_send()
        exit_own(g).wait()
        exit_copy(g).wait()

    def drain(k):
        a2a(k).wait_send()
        final(k).wait_send()
        for layer in range(layers):
            gather(layer, k).wait_send()
            scatter(layer, k).wait_send()

    loop(drain)
    for layer in range(layers):
        cross(layer).wait_send()
        term_copy(layer).wait_send()


def fast_body(angles, depth_order, slices, cotangent):
    count = lax.axis_size("illum")
    _, rows, cols = slices.shape
    groups = cotangent.shape[0]
    held = groups // 2
    layers = depth_order.shape[0]
    width = cols // count
    dma = pltpu.SemaphoreType.DMA
    f32 = jnp.float32
    wave = pltpu.VMEM((held, 2, 2 * rows, cols), f32)
    plane = pltpu.VMEM((layers, 2 * rows, cols), f32)
    half_plane = pltpu.VMEM((layers, rows, cols), f32)
    vmem = pl.BlockSpec(memory_space=pltpu.VMEM)
    smem = pl.BlockSpec(memory_space=pltpu.SMEM)
    out, grad = pl.pallas_call(
        functools.partial(fused, count),
        out_shape=(
            jax.ShapeDtypeStruct(cotangent.shape, f32),
            jax.ShapeDtypeStruct((rows, cols), f32),
        ),
        in_specs=[smem, smem, vmem, vmem],
        out_specs=(pl.BlockSpec(memory_space=pl.ANY), vmem),
        scratch_shapes=[
            pltpu.VMEM((held, 2, 2 * rows, cols + 2 * PAD), f32),
            wave, wave, wave, wave,
            plane, plane, plane, plane, half_plane, half_plane,
            pltpu.VMEM((count, rows, width), f32),
            pltpu.VMEM((layers, count, rows, width), f32),
            pltpu.VMEM((3, rows, width), f32),
            pltpu.VMEM((rows, cols), f32),
            pltpu.VMEM((layers, rows, width), f32),
            dma((held,)), dma((held,)), dma((held,)),
            dma((count,)), dma((count,)),
            dma((layers, count)), dma((layers, count)),
            dma((layers,)), dma((layers,)),
            dma((layers,)), dma((layers,)),
            dma((layers, count)), dma((layers, count)),
            dma((count,)), dma((count,)),
            dma((held,)), dma((held,)), dma((held,)),
        ],
        compiler_params=pltpu.CompilerParams(
            collective_id=0, has_side_effects=True, vmem_limit_bytes=40 * 1024 * 1024
        ),
    )(angles, depth_order, slices[0], cotangent)
    return out, grad[None]


def chosen_body(angles, depth_order, slices, cotangent):
    count = lax.axis_size("illum")
    _, rows, cols = slices.shape
    fits = (
        lax.axis_size("row") == 2
        and rows == 8
        and slices.shape[0] == 1
        and count >= 3
        and cotangent.shape[0] % 2 == 0
        and depth_order.shape[0] == 3
        and cols & (cols - 1) == 0
        and cols % (128 * count) == 0
        and cols % 512 == 0
    )
    run = fast_body if fits else body
    return run(angles, depth_order, slices, cotangent)


def solution(mesh):
    placed = (P("illum", None), P(), P("illum", "row", None), P("illum", None, "row", None))
    return jax.shard_map(
        chosen_body,
        mesh=mesh,
        in_specs=placed,
        out_specs=(P("illum", None, "row", None), P("illum", "row", None)),
        check_vma=False,
    )
```

```python
import functools
import math

import jax
import jax.numpy as jnp
from jax import lax
from jax.experimental import pallas as pl
from jax.experimental.pallas import tpu as pltpu
from jax.sharding import PartitionSpec as P

rate_scale = 0.3


def extended(array, sides, width):
    for axis, dim in sides:
        peers, length = (lax.axis_size(axis), array.shape[dim])
        up = [(i, (i + 1) % peers) for i in range(peers - 1)]
        down = [(j, i) for i, j in up]
        last = lax.slice_in_dim(array, length - width, length, axis=dim)
        initial = lax.slice_in_dim(array, 0, width, axis=dim)
        before = lax.ppermute(last, axis, up)
        after = lax.ppermute(initial, axis, down)
        array = jnp.concatenate([before, array, after], axis=dim)
    return array


def broadcast(block, axis, holder):
    block = jnp.where(lax.axis_index(axis) == holder, block, jnp.zeros_like(block))
    return lax.psum(block, axis)


def laplace_whole(field):
    framed = jnp.pad(field, ((0, 0), (0, 0), (1, 1), (1, 1)))
    return (
        framed[:, :, 2:, 1:-1]
        + framed[:, :, :-2, 1:-1]
        + (framed[:, :, 1:-1, 2:] + framed[:, :, 1:-1, :-2])
        - 4.0 * field
    )


def deep_runge(field, factor, valid):
    padded = extended(field, (("row", 2),), 4)

    def slope(state):
        curved = laplace_whole(state)
        return jnp.stack([-factor * curved[:, 1], factor * curved[:, 0]], axis=1) * valid

    slope_one = slope(padded)
    slope_two = slope(padded + 0.5 * slope_one)
    slope_three = slope(padded + 0.5 * slope_two)
    slope_four = slope(padded + slope_three)
    total = padded + (slope_one + 2.0 * slope_two + 2.0 * slope_three + slope_four) / 6.0
    return total[:, :, 4:-4]


def rotate(field, phase):
    cosine = jnp.cos(phase)
    sine = jnp.sin(phase)
    real_part = field[:, 0]
    imag_part = field[:, 1]
    return jnp.stack(
        [cosine * real_part - sine * imag_part, sine * real_part + cosine * imag_part], axis=1
    )


def inner_term(adjoint, stored):
    return jnp.sum(-adjoint[:, 0] * stored[:, 1] + adjoint[:, 1] * stored[:, 0], axis=0)


def body(angles, depth_order, slices, cotangent):
    rows = slices.shape[1]
    cols = slices.shape[2]
    layers = depth_order.shape[0]
    owner_count = lax.axis_size("illum")
    total_rows = rows * lax.axis_size("row")
    first_row = lax.axis_index("row") * rows
    rows_idx = first_row + jnp.arange(rows, dtype=jnp.int32)
    cols_idx = jnp.arange(cols, dtype=jnp.int32)
    phase_rows = (
        2.0
        * math.pi
        * (angles[:, 0:1] * rows_idx[None, :] % total_rows).astype(jnp.float32)
        / total_rows
    )
    phase_cols = (
        2.0 * math.pi * (angles[:, 1:2] * cols_idx[None, :] % cols).astype(jnp.float32) / cols
    )
    phase = phase_rows[:, :, None] + phase_cols[:, None, :]
    field = jnp.stack([jnp.cos(phase), jnp.sin(phase)], axis=1)
    chosen = [broadcast(slices[0], "illum", depth_order[layer]) for layer in range(layers)]
    kept = [None] * layers
    terms = [None] * layers
    adjoint = cotangent
    wide_idx = first_row - 4 + jnp.arange(rows + 8, dtype=jnp.int32)
    valid = ((wide_idx >= 0) & (wide_idx < total_rows)).astype(jnp.float32)[:, None]
    for layer in range(layers):
        field = rotate(field, chosen[layer])
        kept[layer] = field
        field = deep_runge(field, rate_scale, valid)
    for layer in range(layers - 1, -1, -1):
        adjoint = deep_runge(adjoint, -rate_scale, valid)
        terms[layer] = inner_term(adjoint, kept[layer])
        adjoint = rotate(adjoint, -chosen[layer])
    grads = jnp.stack(terms, axis=0)
    owners = jnp.arange(owner_count, dtype=jnp.int32)
    buffer = jnp.zeros((owner_count, rows, cols), jnp.float32)
    for layer in range(layers):
        picked = (owners == depth_order[layer]).astype(jnp.float32)
        buffer = buffer + picked[:, None, None] * grads[layer][None]
    slice_grad = lax.psum_scatter(buffer, "illum", scatter_dimension=0, tiled=True)
    return (field, slice_grad)


MESH = pl.DeviceIdType.MESH
PAD = 128
STRIP = 4096


def sincos(x):
    k = jnp.floor(x * (2.0 / math.pi) + 0.5)
    r = x - k * 1.5703125
    r = r - k * 4.837512969970703125e-4
    r = r - k * 7.54978995489188e-8
    z = r * r
    s = r + r * z * (-1.6666654611e-1 + z * (8.3321608736e-3 - z * 1.9515295891e-4))
    c = 1.0 - 0.5 * z + z * z * (
        4.166664568298827e-2 + z * (-1.388731625493765e-3 + z * 2.443315711809948e-5)
    )
    q = k.astype(jnp.int32) & 3
    odd = (q & 1) == 1
    sin_mag = jnp.where(odd, c, s)
    cos_mag = jnp.where(odd, s, c)
    sine = jnp.where(q >= 2, -sin_mag, sin_mag)
    cosine = jnp.where((q == 1) | (q == 2), -cos_mag, cos_mag)
    return sine, cosine


def propagate(source, target, g, factor, cols):
    wide = STRIP + 2 * PAD
    sub = lax.broadcasted_iota(jnp.int32, (8, wide), 0)
    lane = lax.broadcasted_iota(jnp.int32, (8, wide), 1)
    first, final = sub == 0, sub == 7
    second = factor * factor / 2.0
    third = factor * factor * factor / 6.0
    fourth = factor * factor * factor * factor / 24.0
    mid = slice(PAD, PAD + STRIP)

    def strip(j, carry):
        start = pl.multiple_of(j * STRIP, STRIP)
        col = lane + (start - PAD)
        inside = jnp.where((col >= 0) & (col < cols), 1.0, 0.0).astype(jnp.float32)

        def curved(t, b):
            rt, rb = pltpu.roll(t, 1, 0), pltpu.roll(b, 1, 0)
            qt, qb = pltpu.roll(t, 7, 0), pltpu.roll(b, 7, 0)
            vt = jnp.where(first, 0.0, rt) + jnp.where(final, qb, qt)
            vb = jnp.where(first, rt, rb) + jnp.where(final, 0.0, qb)
            ht = pltpu.roll(t, 1, 1) + pltpu.roll(t, wide - 1, 1)
            hb = pltpu.roll(b, 1, 1) + pltpu.roll(b, wide - 1, 1)
            return (vt + ht) - 4.0 * t, (vb + hb) - 4.0 * b

        evens, odds = [], []
        for part in range(2):
            u0 = source[g, part, 0:8, pl.ds(start, wide)]
            u1 = source[g, part, 8:16, pl.ds(start, wide)]
            a0, a1 = curved(u0, u1)
            a0, a1 = a0 * inside, a1 * inside
            b0, b1 = curved(a0, a1)
            b0, b1 = b0 * inside, b1 * inside
            even = [u[:, mid] - second * b[:, mid] for u, b in ((u0, b0), (u1, b1))]
            c0, c1 = curved(b0, b1)
            c0, c1 = c0 * inside, c1 * inside
            odd = [factor * a[:, mid] - third * c[:, mid] for a, c in ((a0, c0), (a1, c1))]
            d0, d1 = curved(c0, c1)
            even = [e + fourth * d[:, mid] for e, d in zip(even, (d0, d1))]
            evens.append(even)
            odds.append(odd)
        for half in range(2):
            at = slice(8 * half, 8 * half + 8)
            target[g, 0, at, pl.ds(start, STRIP)] = evens[0][half] - odds[1][half]
            target[g, 1, at, pl.ds(start, STRIP)] = evens[1][half] + odds[0][half]
        return carry

    lax.fori_loop(0, cols // STRIP, strip, 0)


def fused(
    count, angles, order, slices, cot, out, grad,
    tmp, w2, w1, w0, field, full, sine, cosine, term, got, total, parts, rs, picks, gfull, pieces,
    cot_send, cot_recv, cot_local, a2a_send, a2a_recv, a2a_local, ag_send, ag_recv, cx_send, cx_recv,
    tx_send, tx_recv, rs_send, rs_recv, fin_send, fin_recv, ex_send, ex_recv, ex_local,
):
    n = count
    me = lax.axis_index("illum")
    core = lax.axis_index("row")
    other = 1 - core
    cols = slices.shape[1]
    width = cols // n
    held = cot.shape[0] // 2
    layers = full.shape[0]
    mine_rows = pl.ds(pl.multiple_of(core * 8, 8), 8)
    other_rows = pl.ds(pl.multiple_of(other * 8, 8), 8)
    my_cols = pl.ds(pl.multiple_of(me * width, width), width)

    def peer(k):
        return lax.rem(me + k, n)

    def piece(k):
        return pl.ds(pl.multiple_of(k * width, width), width)

    def loop(body):
        def step(k, carry):
            body(k)
            return carry

        lax.fori_loop(1, n, step, 0)

    barrier = pltpu.get_barrier_semaphore()
    loop(lambda k: pl.semaphore_signal(barrier, inc=1, device_id=(peer(k), core), device_id_type=MESH))
    pl.semaphore_signal(barrier, inc=1, device_id=(me, other), device_id_type=MESH)
    pl.semaphore_wait(barrier, n)

    def remote(src, dst, send, recv, where):
        return pltpu.make_async_remote_copy(
            src_ref=src, dst_ref=dst, send_sem=send, recv_sem=recv,
            device_id=where, device_id_type=MESH,
        )

    inner = pl.ds(PAD, cols)

    def cot_copy(g):
        return remote(
            cot.at[other * held + g], tmp.at[g, :, mine_rows, inner],
            cot_send.at[g], cot_recv.at[g], (me, other),
        )

    def cot_own(g):
        return pltpu.make_async_copy(
            cot.at[core * held + g], tmp.at[g, :, mine_rows, inner], cot_local.at[g]
        )

    def a2a(k):
        return remote(
            slices.at[:, piece(peer(k))], parts.at[me], a2a_send.at[k], a2a_recv.at[k],
            (peer(k), core),
        )

    def a2a_own():
        return pltpu.make_async_copy(slices.at[:, my_cols], parts.at[me], a2a_local)

    def gather(layer, k):
        return remote(
            pieces.at[layer], full.at[layer, mine_rows, my_cols],
            ag_send.at[layer, k], ag_recv.at[layer, k], (peer(k), core),
        )

    def cross(layer):
        return remote(
            full.at[layer, mine_rows], full.at[layer, mine_rows],
            cx_send.at[layer], cx_recv.at[layer], (me, other),
        )

    def term_copy(layer):
        return remote(
            term.at[layer, other_rows], got.at[layer],
            tx_send.at[layer], tx_recv.at[layer], (me, other),
        )

    def scatter(layer, k):
        return remote(
            total.at[layer, :, piece(peer(k))], rs.at[layer, k],
            rs_send.at[layer, k], rs_recv.at[layer, k], (peer(k), core),
        )

    def final(k):
        to = peer(k)
        which = (to + n - 2) // (n - 1) + to // (n - 1)
        return remote(
            picks.at[which], gfull.at[:, my_cols], fin_send.at[k], fin_recv.at[k], (to, core)
        )

    def exit_copy(g):
        return remote(
            field.at[g, :, other_rows], out.at[core * held + g],
            ex_send.at[g], ex_recv.at[g], (me, other),
        )

    def exit_own(g):
        return pltpu.make_async_copy(
            field.at[g, :, mine_rows], out.at[core * held + g], ex_local.at[g]
        )

    for g in range(held):
        cot_copy(g).start()
        cot_own(g).start()
    loop(lambda k: a2a(k).start())
    a2a_own().start()
    for g in range(held):
        for part in range(2):
            tmp[g, part, :, 0:PAD] = jnp.zeros((16, PAD), jnp.float32)
            tmp[g, part, :, PAD + cols : 2 * PAD + cols] = jnp.zeros((16, PAD), jnp.float32)

    def back_first(g):
        cot_copy(g).wait_recv()
        cot_own(g).wait()
        propagate(tmp, w2, g, -rate_scale, cols)

    back_first(0)
    loop(lambda k: a2a(k).wait_recv())
    a2a_own().wait()
    for layer in range(layers - 1, -1, -1):
        value = parts[order[layer]]
        pieces[layer] = value
        full[layer, mine_rows, my_cols] = value
        loop(lambda k: gather(layer, k).start())
    for g in range(1, held):
        back_first(g)

    def fetch(layer):
        loop(lambda k: gather(layer, k).wait_recv())
        cross(layer).start()

    tile = 512

    def columns(body):
        def step(j, carry):
            body(pl.multiple_of(j * tile, tile))
            return carry

        lax.fori_loop(0, cols // tile, step, 0)

    def back_turn(layer, waves):
        def body(start):
            at = pl.ds(start, tile)
            to = pl.ds(start + PAD, tile)
            s, c = sincos(full[layer, :, at])
            sine[layer, :, at] = s
            cosine[layer, :, at] = c
            for g in range(held):
                a, b = waves[g, 0, :, at], waves[g, 1, :, at]
                tmp[g, 0, :, to] = a * c + b * s
                tmp[g, 1, :, to] = b * c - a * s

        columns(body)

    fetch(2)
    cross(2).wait_recv()
    fetch(1)
    back_turn(2, w2)
    for g in range(held):
        propagate(tmp, w1, g, -rate_scale, cols)
    cross(1).wait_recv()
    fetch(0)
    back_turn(1, w1)
    for g in range(held):
        propagate(tmp, w0, g, -rate_scale, cols)
    cross(0).wait_recv()

    def first_turn(start):
        at = pl.ds(start, tile)
        to = pl.ds(start + PAD, tile)
        phase = full[0, :, at]
        row = lax.broadcasted_iota(jnp.int32, (16, tile), 0)
        col = lax.broadcasted_iota(jnp.int32, (16, tile), 1) + start
        acc = None
        for g in range(held):
            p = angles[core * held + g, 0]
            q = angles[core * held + g, 1]
            turn = ((row * p) & 15).astype(jnp.float32) * (2.0 * math.pi / 16)
            turn = turn + ((col * q) & (cols - 1)).astype(jnp.float32) * (2.0 * math.pi / cols)
            s, c = sincos(turn + phase)
            tmp[g, 0, :, to] = c
            tmp[g, 1, :, to] = s
            piece_sum = w0[g, 1, :, at] * c - w0[g, 0, :, at] * s
            acc = piece_sum if acc is None else acc + piece_sum
        term[0, :, at] = acc

    def turn(layer, waves):
        def body(start):
            at = pl.ds(start, tile)
            to = pl.ds(start + PAD, tile)
            s, c = sine[layer, :, at], cosine[layer, :, at]
            acc = None
            for g in range(held):
                a, b = field[g, 0, :, at], field[g, 1, :, at]
                real = a * c - b * s
                imag = a * s + b * c
                tmp[g, 0, :, to] = real
                tmp[g, 1, :, to] = imag
                piece_sum = waves[g, 1, :, at] * real - waves[g, 0, :, at] * imag
                acc = piece_sum if acc is None else acc + piece_sum
            term[layer, :, at] = acc

        columns(body)

    def spread(layer):
        term_copy(layer).wait_recv()
        total[layer] = term[layer, mine_rows] + got[layer]
        loop(lambda k: scatter(layer, k).start())

    columns(first_turn)
    term_copy(0).start()
    propagate(tmp, field, 0, rate_scale, cols)
    spread(0)
    for g in range(1, held):
        propagate(tmp, field, g, rate_scale, cols)
    turn(1, w1)
    term_copy(1).start()
    propagate(tmp, field, 0, rate_scale, cols)
    spread(1)
    for g in range(1, held):
        propagate(tmp, field, g, rate_scale, cols)
    turn(2, w2)
    term_copy(2).start()
    propagate(tmp, field, 0, rate_scale, cols)
    spread(2)
    exit_copy(0).start()
    exit_own(0).start()
    for g in range(1, held):
        propagate(tmp, field, g, rate_scale, cols)
        exit_copy(g).start()
        exit_own(g).start()

    sums = []
    for layer in range(layers):
        loop(lambda k: scatter(layer, k).wait_recv())
        acc = total[layer, :, my_cols]
        for k in range(1, n):
            acc = acc + rs[layer, k]
        sums.append(acc)
    zero = jnp.zeros_like(sums[0])
    low = zero
    high = zero
    middle = zero
    for layer in range(layers):
        place = order[layer]
        low = low + jnp.where(place == 0, sums[layer], zero)
        high = high + jnp.where(place == n - 1, sums[layer], zero)
        middle = middle + jnp.where((place > 0) & (place < n - 1), sums[layer], zero)
    picks[0] = low
    picks[1] = middle
    picks[2] = high
    loop(lambda k: final(k).start())
    gfull[:, my_cols] = picks[(me + n - 2) // (n - 1) + me // (n - 1)]
    named = (order[0] == me) | (order[1] == me) | (order[2] == me)
    loop(lambda k: final(k).wait_recv())
    value = gfull[...]
    grad[...] = jnp.where(named, value, jnp.zeros_like(value))

    for g in range(held):
        cot_copy(g).wait_send()
        exit_own(g).wait()
        exit_copy(g).wait()

    def drain(k):
        a2a(k).wait_send()
        final(k).wait_send()
        for layer in range(layers):
            gather(layer, k).wait_send()
            scatter(layer, k).wait_send()

    loop(drain)
    for layer in range(layers):
        cross(layer).wait_send()
        term_copy(layer).wait_send()


def fast_body(angles, depth_order, slices, cotangent):
    count = lax.axis_size("illum")
    _, rows, cols = slices.shape
    groups = cotangent.shape[0]
    held = groups // 2
    layers = depth_order.shape[0]
    width = cols // count
    dma = pltpu.SemaphoreType.DMA
    f32 = jnp.float32
    wave = pltpu.VMEM((held, 2, 2 * rows, cols), f32)
    plane = pltpu.VMEM((layers, 2 * rows, cols), f32)
    half_plane = pltpu.VMEM((layers, rows, cols), f32)
    vmem = pl.BlockSpec(memory_space=pltpu.VMEM)
    smem = pl.BlockSpec(memory_space=pltpu.SMEM)
    out, grad = pl.pallas_call(
        functools.partial(fused, count),
        out_shape=(
            jax.ShapeDtypeStruct(cotangent.shape, f32),
            jax.ShapeDtypeStruct((rows, cols), f32),
        ),
        in_specs=[smem, smem, pl.BlockSpec(memory_space=pl.ANY), pl.BlockSpec(memory_space=pl.ANY)],
        out_specs=(pl.BlockSpec(memory_space=pl.ANY), vmem),
        scratch_shapes=[
            pltpu.VMEM((held, 2, 2 * rows, cols + 2 * PAD), f32),
            wave, wave, wave, wave,
            plane, plane, plane, plane, half_plane, half_plane,
            pltpu.VMEM((count, rows, width), f32),
            pltpu.VMEM((layers, count, rows, width), f32),
            pltpu.VMEM((3, rows, width), f32),
            pltpu.VMEM((rows, cols), f32),
            pltpu.VMEM((layers, rows, width), f32),
            dma((held,)), dma((held,)), dma((held,)),
            dma((count,)), dma((count,)), dma(()),
            dma((layers, count)), dma((layers, count)),
            dma((layers,)), dma((layers,)),
            dma((layers,)), dma((layers,)),
            dma((layers, count)), dma((layers, count)),
            dma((count,)), dma((count,)),
            dma((held,)), dma((held,)), dma((held,)),
        ],
        compiler_params=pltpu.CompilerParams(
            collective_id=0, has_side_effects=True, vmem_limit_bytes=56 * 1024 * 1024
        ),
    )(angles, depth_order, slices[0], cotangent)
    return out, grad[None]


def chosen_body(angles, depth_order, slices, cotangent):
    count = lax.axis_size("illum")
    _, rows, cols = slices.shape
    fits = (
        lax.axis_size("row") == 2
        and rows == 8
        and slices.shape[0] == 1
        and count >= 3
        and cotangent.shape[0] % 2 == 0
        and depth_order.shape[0] == 3
        and cols & (cols - 1) == 0
        and cols % (128 * count) == 0
        and cols % STRIP == 0
    )
    run = fast_body if fits else body
    return run(angles, depth_order, slices, cotangent)


def solution(mesh):
    placed = (P("illum", None), P(), P("illum", "row", None), P("illum", None, "row", None))
    return jax.shard_map(
        chosen_body,
        mesh=mesh,
        in_specs=placed,
        out_specs=(P("illum", None, "row", None), P("illum", "row", None)),
        check_vma=False,
    )
```
